32 devices in a mesh: groups: 2 (over x), layer: 8 (over z, y), ex: 2 (over core).
Axes of the slice: x: 2, y: 2, z: 4, core: 2. Of those that a mesh axis runs over, the one named last changes fastest.
Arguments:
- query_grads: bfloat16 [128, 8, 4096], P(('groups', 'layer')), parts along dimension 0, may hold values from -9000 to 9000
- inv_in: bfloat16 [8, 64, 64], P('layer'), may hold values from -0.4 to 3, as said below
- inv_out: bfloat16 [8, 64, 64], P('layer'), may hold values from -0.4 to 3, as said below
- train_grads: bfloat16 [8, 6144, 4096], P('layer', ('groups', 'ex')), parts along dimension 1, may hold values from -6 to 6
Outputs:
- scores: float32 [64, 6144], P('layer', ('groups', 'ex')), parts along dimension 1
The draws below stay inside these ranges and needn't reach their ends.
There are 2 independent parts, one for each index of `groups`. The reference program is written for one: setup_inputs(seed, part) draws one part's arguments, and reference() takes and returns one part's arrays. A program takes and returns all parts, laid end to end along the dimension named above; an argument that names none is the same for every part. Nothing has to cross between parts.
Inputs may be any that keep to these rules, and one draw needn't show every extreme that they name: `inv_in`: each matrix is symmetric positive definite. `inv_out`: each matrix is symmetric positive definite.
All inputs are finite; a program needn't handle non-finite values.
Results may differ from the reference program's by a relative error of at most 0.0042.
Values may be sent and summed in bfloat16 or wider, within the bound.
A program may use at most 64 MiB of HBM per device.

```python
import math
import jax
import jax.numpy as jnp
from jax import lax

KI = 64
KO = 64
P_SIZE = 4096
Q = 64
EX = 3072
MODULES = 8


def draw_query_grads(key, part):
    key = jax.random.fold_in(key, 11)
    first_key, second_key, third_key = jax.random.split(key, 3)
    module_pos = jnp.arange(MODULES, dtype=jnp.float32) / max(MODULES - 1, 1)
    base = jax.random.truncated_normal(first_key, -4.0, 4.0, (Q, MODULES, P_SIZE), jnp.float32)
    rising = 3.0 ** module_pos
    row_scale = jnp.exp(jax.random.uniform(second_key, (Q, 1, 1), jnp.float32, 0.0, math.log(10.0)))
    column_scale = jnp.exp(jax.random.uniform(third_key, (1, MODULES, P_SIZE), jnp.float32, 0.0, math.log(10.0)))
    return (base * rising[None, :, None] * row_scale * column_scale).astype(jnp.bfloat16)


def draw_factor(key, width, off_scale, lowest, highest):
    first_key, second_key = jax.random.split(key)
    offdiag = jax.random.truncated_normal(first_key, -4.0, 4.0, (MODULES, width, width), jnp.float32) * off_scale
    symmetric = (offdiag + jnp.swapaxes(offdiag, 1, 2)) * 0.7071
    diagonal = jax.random.uniform(second_key, (MODULES, width, 1), jnp.float32, lowest, highest)
    identity = jnp.eye(width, dtype=jnp.float32)
    return (symmetric * (1.0 - identity) + diagonal * identity).astype(jnp.bfloat16)


def draw_inv_in(key, part):
    key = jax.random.fold_in(key, 23)
    return draw_factor(key, KI, 0.05, 1.0, 2.5)


def draw_inv_out(key, part):
    key = jax.random.fold_in(key, 37)
    return draw_factor(key, KO, 0.05, 1.0, 2.5)


def steps_of(own_key, dims, cuts, smallest, largest):
    def one(position, parts):
        steps = jax.random.uniform(jax.random.fold_in(jax.random.fold_in(own_key, 6), position), (parts,), jnp.float32, smallest / len(cuts), largest / len(cuts))
        return jnp.repeat(jnp.exp(steps), dims[position] // parts).reshape((-1,) + (1,) * (len(dims) - position - 1))

    level = one(*cuts[0])
    for cut in cuts[1:]:
        level = level * one(*cut)
    return level


def noise(stream_key, shape, scale, most, shards=(), kind=jnp.bfloat16):
    values = scale * jax.random.normal(stream_key, shape, jnp.float32)
    if shards:
        values = values * steps_of(stream_key, shape, shards, -0.22, 0.18)
    return jnp.clip(values, -most, most).astype(kind)


def setup_inputs(seed: int = 0, part: int = 0) -> dict:
    arg_keys = jax.random.split(jax.random.key(seed), 5)
    part_keys = jax.random.split(jax.random.fold_in(arg_keys[4], part), 5)
    return {
        "query_grads": draw_query_grads(jax.random.fold_in(jax.random.fold_in(arg_keys[4], part), 71), part),
        "inv_in": draw_inv_in(jax.random.fold_in(arg_keys[4], 71), part),
        "inv_out": draw_inv_out(jax.random.fold_in(arg_keys[4], 71), part),
        "train_grads": noise(part_keys[3], (MODULES, EX, P_SIZE), 1.0, 6.0, ((0, 8), (1, 2))),
    }


epsilon = 1e-06

def condition(gradients, left_factor, right_factor):
    picked, modules, length = gradients.shape
    inner_dim = left_factor.shape[-1]
    outer_dim = right_factor.shape[-1]
    shaped = gradients.reshape(picked, modules, inner_dim, outer_dim).astype(jnp.float32)
    mixed_rows = jnp.einsum('mij,rmjk->rmik', left_factor.astype(jnp.float32), shaped, precision=lax.Precision.HIGHEST).astype(jnp.bfloat16)
    result = jnp.einsum('rmik,mkl->rmil', mixed_rows.astype(jnp.float32), right_factor.astype(jnp.float32), precision=lax.Precision.HIGHEST).astype(jnp.bfloat16)
    return result.reshape(picked, modules, length)

def reference(query_grads, inv_in, inv_out, train_grads):
    conditioned = condition(query_grads, inv_in, inv_out)
    widened = conditioned.astype(jnp.float32)
    norms = lax.optimization_barrier(jnp.sum(widened * widened, axis=(1, 2)))
    swapped = jnp.swapaxes(conditioned, 0, 1)

    def add_module(total, pieces):
        query_part, train_part = pieces
        return (total + lax.dot_general(query_part, train_part, (((1,), (1,)), ((), ())), preferred_element_type=jnp.float32), None)
    start_total = jnp.zeros((query_grads.shape[0], train_grads.shape[1]), jnp.float32)
    summed, _ = lax.scan(add_module, start_total, (swapped, train_grads))
    return summed / jnp.sqrt(norms + epsilon)[:, None]
```

```python
import math

import jax
import jax.numpy as jnp
from jax import lax
from jax.experimental import pallas as pl
from jax.experimental.pallas import tpu as pltpu
from jax.sharding import PartitionSpec as P

epsilon = 1e-06
LANES = 128
CHUNK = 16
BLOCKS = 2
MESH = pl.DeviceIdType.MESH
F32 = jnp.float32
BF16 = jnp.bfloat16


def iota(shape, dim):
    return lax.broadcasted_iota(jnp.int32, shape, dim)


def dot(a, b):
    return jnp.dot(a, b, preferred_element_type=F32)


def dot_nt(a, b):
    return lax.dot_general(a, b, (((1,), (1,)), ((), ())), preferred_element_type=F32)


def stack(pieces, axis=0):
    return pieces[0] if len(pieces) == 1 else jnp.concatenate(pieces, axis=axis)


def left_weights(factor):
    size = factor.shape[0]
    half = size // 2
    row, col = iota((size, size), 0), iota((size, size), 1)
    low = row < half
    even_first = jnp.where(low, 2 * row, 2 * (row - half) + 1)
    odd_first = jnp.where(low, 2 * row + 1, 2 * (row - half))
    order = (col == even_first).astype(F32).astype(BF16)
    swapped = (col == odd_first).astype(F32).astype(BF16)
    rows = dot(order, factor).astype(BF16)
    return jnp.where(low, dot_nt(rows, order), dot_nt(rows, swapped)).astype(BF16)


def right_weights(factor):
    size = factor.shape[0]
    row, col = iota((2 * size, size), 0), iota((2 * size, size), 1)
    spread = ((row == col) | (row == col + size)).astype(F32).astype(BF16)
    tiled = dot_nt(dot(spread, factor).astype(BF16), spread)
    row, col = iota((2 * size, 2 * size), 0), iota((2 * size, 2 * size), 1)
    return jnp.where((row < size) == (col < size), tiled, 0.0).astype(BF16)


def kernel(
    layers, own, dims,
    query_hbm, left_hbm, right_hbm, train_hbm,
    out_ref,
    query_v, left_v, right_v, train_v, wide, slabs, arrived, plain, cond, scores, sent, got, norm_sent, norm_got,
    local_sem, train_sem, q_send, q_recv, c_send, c_recv, s_send, s_recv, n_send, n_recv,
):
    groups, slots, per_chunk, chunks, rows_all, block, fold, width, slab_rows = dims
    me = lax.axis_index("layer")
    core = lax.axis_index("ex")

    loads = [
        pltpu.make_async_copy(query_hbm, query_v, local_sem.at[0]),
        pltpu.make_async_copy(left_hbm, left_v, local_sem.at[1]),
        pltpu.make_async_copy(right_hbm, right_v, local_sem.at[2]),
    ]
    for load in loads:
        load.start()
    train_loads = [
        pltpu.make_async_copy(train_hbm.at[pl.ds(b * block, block)], train_v.at[b], train_sem.at[b])
        for b in range(BLOCKS)
    ]

    barrier = pltpu.get_barrier_semaphore()
    for k in range(1, layers):
        pl.semaphore_signal(
            barrier, inc=1, device_id={"layer": lax.rem(me + k, layers)}, device_id_type=MESH
        )
    pl.semaphore_signal(barrier, inc=1, device_id={"ex": 1 - core}, device_id_type=MESH)

    loads[0].wait()
    for load in train_loads:
        load.start()
    for r in range(own):
        row = query_v[r].astype(F32)
        for t in range(groups):
            wide[r, pl.ds(t, layers, stride=groups), :] = row[:, t * LANES:(t + 1) * LANES]

    def query_copy(i):
        return pltpu.make_async_remote_copy(
            src_ref=slabs.at[i],
            dst_ref=arrived.at[i],
            send_sem=q_send.at[i],
            recv_sem=q_recv.at[i],
            device_id={"layer": lax.rem(me + 2 * i + core, layers)},
            device_id_type=MESH,
        )

    def slab_of(i):
        target = lax.rem(me + 2 * i + core, layers)
        start = pl.multiple_of(target * groups, groups)
        return stack([wide[r, pl.ds(start, groups), :] for r in range(own)], axis=1).astype(BF16)

    for i in range(slots):
        slabs[i] = slab_of(i)
        if i == 0:
            pl.semaphore_wait(barrier, layers)

            @pl.when(core == 0)
            def _():
                arrived[0] = slabs[0]

            @pl.when(core != 0)
            def _():
                query_copy(0).start()
        else:
            query_copy(i).start()

    loads[1].wait()
    loads[2].wait()
    left = left_weights(left_v[0])
    right = right_weights(right_v[0])
    low = iota((groups, LANES), 1) < LANES // 2

    def cond_copy(j):
        place = core * chunks + j
        return pltpu.make_async_remote_copy(
            src_ref=cond.at[place],
            dst_ref=cond.at[place],
            send_sem=c_send.at[j],
            recv_sem=c_recv.at[j],
            device_id={"ex": 1 - core},
            device_id_type=MESH,
        )

    for j in range(chunks):
        pieces = []
        for i in range(j * per_chunk, (j + 1) * per_chunk):
            if i == 0:
                @pl.when(core != 0)
                def _():
                    query_copy(0).wait_recv()
            else:
                query_copy(i).wait_recv()
            slab = arrived[i].astype(F32)
            for r in range(own):
                piece = slab[:, r * LANES:(r + 1) * LANES]
                pieces.append(stack([piece, pltpu.roll(piece, LANES // 2, 1)], axis=0))
        both = dot(left, stack(pieces, axis=1).astype(BF16))
        mixed = stack(
            [
                jnp.where(low, both[:groups, n * LANES:(n + 1) * LANES], both[groups:, n * LANES:(n + 1) * LANES])
                for n in range(CHUNK)
            ],
            axis=0,
        ).astype(BF16)
        plain[...] = dot(mixed, right)
        place = core * chunks + j
        for t in range(groups):
            cond[place, :, t * LANES:(t + 1) * LANES] = plain[pl.ds(t, CHUNK, stride=groups), :].astype(BF16)
        cond_copy(j).start()

    for j in range(chunks):
        pltpu.make_async_remote_copy(
            src_ref=cond.at[(1 - core) * chunks + j],
            dst_ref=cond.at[(1 - core) * chunks + j],
            send_sem=c_send.at[j],
            recv_sem=c_recv.at[j],
            device_id={"ex": 1 - core},
            device_id_type=MESH,
        ).wait_recv()

    def rows_of(k):
        return (k % 2) * (rows_all // 2) + (k // 2) * own

    queries = cond[...].reshape(rows_all, groups * LANES)
    total = jnp.zeros((rows_all, LANES), F32)
    for t in range(groups):
        piece = queries[:, t * LANES:(t + 1) * LANES].astype(F32)
        total = total + piece * piece
    norms = jnp.broadcast_to(jnp.sum(total, axis=1, keepdims=True), (rows_all, LANES))

    def norm_copy(k):
        return pltpu.make_async_remote_copy(
            src_ref=norm_sent.at[k],
            dst_ref=norm_got.at[k],
            send_sem=n_send.at[k],
            recv_sem=n_recv.at[k],
            device_id={"layer": lax.rem(me + layers - k, layers)},
            device_id_type=MESH,
        )

    def score_copy(b, k):
        return pltpu.make_async_remote_copy(
            src_ref=sent.at[b, k],
            dst_ref=got.at[b, k],
            send_sem=s_send.at[b, k],
            recv_sem=s_recv.at[b, k],
            device_id={"layer": lax.rem(me + layers - k, layers)},
            device_id_type=MESH,
        )

    for k in range(layers):
        value = norms[rows_of(k):rows_of(k) + own]
        norm_sent[k] = stack([value] * max(1, 8 // own), axis=0)
        if k:
            norm_copy(k).start()

    for b in range(BLOCKS):
        train_loads[b].wait()
        scores[b] = dot_nt(cond[...].reshape(rows_all, groups * LANES), train_v[b])
        for k in range(1, layers):
            value = scores[b, pl.ds(rows_of(k), own), :]
            parts = [value[:, f * width:(f + 1) * width] for f in range(fold)]
            if own * fold < slab_rows:
                parts.append(jnp.zeros((slab_rows - own * fold, width), F32))
            sent[b, k] = stack(parts, axis=0).astype(BF16)
            score_copy(b, k).start()

    norm = norm_sent[0]
    for k in range(1, layers):
        norm_copy(k).wait_recv()
        norm = norm + norm_got[k]
    scale = jnp.sqrt(norm[:own, :1] + epsilon)
    for b in range(BLOCKS):
        summed = jnp.zeros((slab_rows, width), F32)
        for k in range(1, layers):
            score_copy(b, k).wait_recv()
            summed = summed + got[b, k].astype(F32)
        flat = stack([summed[f * own:(f + 1) * own] for f in range(fold)], axis=1)
        out_ref[:, b * block:(b + 1) * block] = (flat + scores[b, pl.ds(0, own), :]) / scale

    for i in range(slots):
        if i == 0:
            @pl.when(core != 0)
            def _():
                query_copy(0).wait_send()
        else:
            query_copy(i).wait_send()
    for j in range(chunks):
        cond_copy(j).wait_send()
    for k in range(1, layers):
        norm_copy(k).wait_send()
        for b in range(BLOCKS):
            score_copy(b, k).wait_send()


def per_device(layers, query_grads, inv_in, inv_out, train_grads):
    own, _, length = query_grads.shape
    examples = train_grads.shape[1]
    groups = length // LANES
    slots = layers // 2
    per_chunk = CHUNK // own
    rows_all = own * layers
    chunks = rows_all // 2 // CHUNK
    block = examples // BLOCKS
    fold = math.gcd(max(1, CHUNK // own), block // LANES)
    width = block // fold
    slab_rows = max(CHUNK, own * fold)
    norm_rows = max(8, own)
    dims = (groups, slots, per_chunk, chunks, rows_all, block, fold, width, slab_rows)
    any_space = pl.BlockSpec(memory_space=pltpu.HBM)
    in_vmem = pl.BlockSpec(memory_space=pltpu.VMEM)
    dma = pltpu.SemaphoreType.DMA
    return pl.pallas_call(
        lambda *refs: kernel(layers, own, dims, *refs),
        out_shape=jax.ShapeDtypeStruct((own, examples), F32),
        in_specs=[any_space] * 4,
        out_specs=in_vmem,
        scratch_shapes=[
            pltpu.VMEM(query_grads.shape, BF16),
            pltpu.VMEM(inv_in.shape, BF16),
            pltpu.VMEM(inv_out.shape, BF16),
            pltpu.VMEM((BLOCKS, block, length), BF16),
            pltpu.VMEM((own, layers * groups, LANES), F32),
            pltpu.VMEM((slots, groups, own * LANES), BF16),
            pltpu.VMEM((slots, groups, own * LANES), BF16),
            pltpu.VMEM((CHUNK * groups, LANES), F32),
            pltpu.VMEM((2 * chunks, CHUNK, length), BF16),
            pltpu.VMEM((BLOCKS, rows_all, block), F32),
            pltpu.VMEM((BLOCKS, layers, slab_rows, width), BF16),
            pltpu.VMEM((BLOCKS, layers, slab_rows, width), BF16),
            pltpu.VMEM((layers, norm_rows, LANES), F32),
            pltpu.VMEM((layers, norm_rows, LANES), F32),
            dma((3,)),
            dma((BLOCKS,)),
            dma((slots,)),
            dma((slots,)),
            dma((chunks,)),
            dma((chunks,)),
            dma((BLOCKS, layers)),
            dma((BLOCKS, layers)),
            dma((layers,)),
            dma((layers,)),
        ],
        compiler_params=pltpu.CompilerParams(
            collective_id=0, has_side_effects=True, vmem_limit_bytes=60 * 1024 * 1024
        ),
        cost_estimate=pl.CostEstimate(
            flops=2 * rows_all * examples * length, bytes_accessed=2 * examples * length, transcendentals=0
        ),
    )(query_grads, inv_in, inv_out, train_grads[0])


def solution(mesh):
    layers = mesh.shape["layer"]
    return jax.shard_map(
        lambda *args: per_device(layers, *args),
        mesh=mesh,
        in_specs=(
            P(("groups", "layer"), None, None),
            P("layer", None, None),
            P("layer", None, None),
            P("layer", ("groups", "ex"), None),
        ),
        out_specs=P("layer", ("groups", "ex")),
        check_vma=False,
    )
```

```python
import math

import jax
import jax.numpy as jnp
from jax import lax
from jax.experimental import pallas as pl
from jax.experimental.pallas import tpu as pltpu
from jax.sharding import PartitionSpec as P

epsilon = 1e-06
LANES = 128
CHUNK = 16
BLOCKS = 3
MESH = pl.DeviceIdType.MESH
F32 = jnp.float32
BF16 = jnp.bfloat16


def iota(shape, dim):
    return lax.broadcasted_iota(jnp.int32, shape, dim)


def dot(a, b):
    return jnp.dot(a, b, preferred_element_type=F32)


def dot_nt(a, b):
    return lax.dot_general(a, b, (((1,), (1,)), ((), ())), preferred_element_type=F32)


def stack(pieces, axis=0):
    return pieces[0] if len(pieces) == 1 else jnp.concatenate(pieces, axis=axis)


def left_weights(factor):
    size = factor.shape[0]
    half = size // 2
    row, col = iota((size, size), 0), iota((size, size), 1)
    low = row < half
    even_first = jnp.where(low, 2 * row, 2 * (row - half) + 1)
    odd_first = jnp.where(low, 2 * row + 1, 2 * (row - half))
    order = (col == even_first).astype(F32).astype(BF16)
    swapped = (col == odd_first).astype(F32).astype(BF16)
    rows = dot(order, factor).astype(BF16)
    return jnp.where(low, dot_nt(rows, order), dot_nt(rows, swapped)).astype(BF16)


def right_weights(factor):
    size = factor.shape[0]
    row, col = iota((2 * size, size), 0), iota((2 * size, size), 1)
    spread = ((row == col) | (row == col + size)).astype(F32).astype(BF16)
    tiled = dot_nt(dot(spread, factor).astype(BF16), spread)
    row, col = iota((2 * size, 2 * size), 0), iota((2 * size, 2 * size), 1)
    return jnp.where((row < size) == (col < size), tiled, 0.0).astype(BF16)


def kernel(
    layers, own, dims,
    query_hbm, left_hbm, right_hbm, train_hbm,
    out_ref,
    query_v, left_v, right_v, train_v, wide, slabs, arrived, plain, cond, scores, sent, got, norm_high, norm_low,
    local_sem, train_sem, q_send, q_recv, c_send, c_recv, s_send, s_recv,
):
    groups, slots, per_chunk, chunks, rows_all, block, fold, width, slab_rows = dims
    me = lax.axis_index("layer")
    core = lax.axis_index("ex")

    loads = [
        pltpu.make_async_copy(query_hbm, query_v, local_sem.at[0]),
        pltpu.make_async_copy(left_hbm, left_v, local_sem.at[1]),
        pltpu.make_async_copy(right_hbm, right_v, local_sem.at[2]),
    ]
    for load in loads:
        load.start()
    train_loads = [
        pltpu.make_async_copy(train_hbm.at[pl.ds(b * block, block)], train_v.at[b], train_sem.at[b])
        for b in range(BLOCKS)
    ]

    barrier = pltpu.get_barrier_semaphore()
    for k in range(1, layers):
        pl.semaphore_signal(
            barrier, inc=1, device_id={"layer": lax.rem(me + k, layers)}, device_id_type=MESH
        )
    pl.semaphore_signal(barrier, inc=1, device_id={"ex": 1 - core}, device_id_type=MESH)

    loads[0].wait()
    for load in train_loads:
        load.start()
    for r in range(own):
        row = query_v[r].astype(F32)
        for t in range(groups):
            wide[r, pl.ds(t, layers, stride=groups), :] = row[:, t * LANES:(t + 1) * LANES]

    def query_copy(i):
        return pltpu.make_async_remote_copy(
            src_ref=slabs.at[i],
            dst_ref=arrived.at[i],
            send_sem=q_send.at[i],
            recv_sem=q_recv.at[i],
            device_id={"layer": lax.rem(me + 2 * i + core, layers)},
            device_id_type=MESH,
        )

    def slab_of(i):
        target = lax.rem(me + 2 * i + core, layers)
        start = pl.multiple_of(target * groups, groups)
        return stack([wide[r, pl.ds(start, groups), :] for r in range(own)], axis=1).astype(BF16)

    for i in range(slots):
        slabs[i] = slab_of(i)
        if i == 0:
            pl.semaphore_wait(barrier, layers)

            @pl.when(core == 0)
            def _():
                arrived[0] = slabs[0]

            @pl.when(core != 0)
            def _():
                query_copy(0).start()
        else:
            query_copy(i).start()

    loads[1].wait()
    loads[2].wait()
    left = left_weights(left_v[0])
    right = right_weights(right_v[0])
    low = iota((groups, LANES), 1) < LANES // 2

    def cond_copy(j):
        place = core * chunks + j
        return pltpu.make_async_remote_copy(
            src_ref=cond.at[place],
            dst_ref=cond.at[place],
            send_sem=c_send.at[j],
            recv_sem=c_recv.at[j],
            device_id={"ex": 1 - core},
            device_id_type=MESH,
        )

    for j in range(chunks):
        pieces = []
        for i in range(j * per_chunk, (j + 1) * per_chunk):
            if i == 0:
                @pl.when(core != 0)
                def _():
                    query_copy(0).wait_recv()
            else:
                query_copy(i).wait_recv()
            slab = arrived[i].astype(F32)
            for r in range(own):
                piece = slab[:, r * LANES:(r + 1) * LANES]
                pieces.append(stack([piece, pltpu.roll(piece, LANES // 2, 1)], axis=0))
        both = dot(left, stack(pieces, axis=1).astype(BF16))
        mixed = stack(
            [
                jnp.where(low, both[:groups, n * LANES:(n + 1) * LANES], both[groups:, n * LANES:(n + 1) * LANES])
                for n in range(CHUNK)
            ],
            axis=0,
        ).astype(BF16)
        plain[...] = dot(mixed, right)
        place = core * chunks + j
        for t in range(groups):
            cond[place, :, t * LANES:(t + 1) * LANES] = plain[pl.ds(t, CHUNK, stride=groups), :].astype(BF16)
        cond_copy(j).start()

    for j in range(chunks):
        pltpu.make_async_remote_copy(
            src_ref=cond.at[(1 - core) * chunks + j],
            dst_ref=cond.at[(1 - core) * chunks + j],
            send_sem=c_send.at[j],
            recv_sem=c_recv.at[j],
            device_id={"ex": 1 - core},
            device_id_type=MESH,
        ).wait_recv()

    def rows_of(k):
        return (k % 2) * (rows_all // 2) + (k // 2) * own

    def score_copy(b, k):
        return pltpu.make_async_remote_copy(
            src_ref=sent.at[b, k, :, pl.ds(0, width + LANES if b == 0 else width)],
            dst_ref=got.at[b, k, :, pl.ds(0, width + LANES if b == 0 else width)],
            send_sem=s_send.at[b],
            recv_sem=s_recv.at[b],
            device_id={"layer": lax.rem(me + layers - k, layers)},
            device_id_type=MESH,
        )

    def wait_all(buffer, b, sem):
        others = buffer.at[b, pl.ds(1, layers - 1), :, pl.ds(0, width + LANES if b == 0 else width)]
        pltpu.make_async_copy(others, others, sem.at[b]).wait()

    for i in range(slots):
        if i == 0:
            @pl.when(core != 0)
            def _():
                query_copy(0).wait_send()
        else:
            query_copy(i).wait_send()

    for b in range(BLOCKS):
        train_loads[b].wait()
        queries = cond[...].reshape(rows_all, groups * LANES)
        scores[b] = dot_nt(queries, train_v[b])
        if b == 0:
            total = jnp.zeros((rows_all, LANES), F32)
            for t in range(groups):
                piece = queries[:, t * LANES:(t + 1) * LANES].astype(F32)
                total = total + piece * piece
            norms = jnp.broadcast_to(jnp.sum(total, axis=1, keepdims=True), (rows_all, LANES))
            high = norms.astype(BF16).astype(F32)
            norm_high[...] = high
            norm_low[...] = norms - high
        for k in range(1, layers):
            rows = pl.ds(rows_of(k), own)
            value = scores[b, rows, :]
            parts = [value[:, f * width:(f + 1) * width] for f in range(fold)]
            if own * fold < slab_rows:
                parts.append(jnp.zeros((slab_rows - own * fold, width), F32))
            sent[b, k, :, :width] = stack(parts, axis=0).astype(BF16)
            if b == 0:
                parts = [norm_high[rows, :], norm_low[rows, :]]
                if own * 2 < slab_rows:
                    parts.append(jnp.zeros((slab_rows - own * 2, LANES), F32))
                sent[b, k, :, width:] = stack(parts, axis=0).astype(BF16)
            score_copy(b, k).start()

    for j in range(chunks):
        cond_copy(j).wait_send()
    for b in range(BLOCKS):
        wait_all(got, b, s_recv)
        if b == 0:
            pair = jnp.zeros((slab_rows, LANES), F32)
            for k in range(1, layers):
                pair = pair + got[0, k, :, width:].astype(F32)
            norm = norm_high[:own] + norm_low[:own] + pair[:own] + pair[own:2 * own]
            scale = jnp.sqrt(norm[:, :1] + epsilon)
        summed = jnp.zeros((slab_rows, width), F32)
        for k in range(1, layers):
            summed = summed + got[b, k, :, :width].astype(F32)
        flat = stack([summed[f * own:(f + 1) * own] for f in range(fold)], axis=1)
        out_ref[:, b * block:(b + 1) * block] = (flat + scores[b, pl.ds(0, own), :]) / scale
        wait_all(sent, b, s_send)


def per_device(layers, query_grads, inv_in, inv_out, train_grads):
    own, _, length = query_grads.shape
    examples = train_grads.shape[1]
    groups = length // LANES
    slots = layers // 2
    per_chunk = CHUNK // own
    rows_all = own * layers
    chunks = rows_all // 2 // CHUNK
    block = examples // BLOCKS
    fold = math.gcd(max(1, CHUNK // own), block // LANES)
    width = block // fold
    slab_rows = max(CHUNK, own * fold, own * 2)
    dims = (groups, slots, per_chunk, chunks, rows_all, block, fold, width, slab_rows)
    any_space = pl.BlockSpec(memory_space=pltpu.HBM)
    in_vmem = pl.BlockSpec(memory_space=pltpu.VMEM)
    dma = pltpu.SemaphoreType.DMA
    return pl.pallas_call(
        lambda *refs: kernel(layers, own, dims, *refs),
        out_shape=jax.ShapeDtypeStruct((own, examples), F32),
        in_specs=[any_space] * 4,
        out_specs=in_vmem,
        scratch_shapes=[
            pltpu.VMEM(query_grads.shape, BF16),
            pltpu.VMEM(inv_in.shape, BF16),
            pltpu.VMEM(inv_out.shape, BF16),
            pltpu.VMEM((BLOCKS, block, length), BF16),
            pltpu.VMEM((own, layers * groups, LANES), F32),
            pltpu.VMEM((slots, groups, own * LANES), BF16),
            pltpu.VMEM((slots, groups, own * LANES), BF16),
            pltpu.VMEM((CHUNK * groups, LANES), F32),
            pltpu.VMEM((2 * chunks, CHUNK, length), BF16),
            pltpu.VMEM((BLOCKS, rows_all, block), F32),
            pltpu.VMEM((BLOCKS, layers, slab_rows, width + LANES), BF16),
            pltpu.VMEM((BLOCKS, layers, slab_rows, width + LANES), BF16),
            pltpu.VMEM((rows_all, LANES), F32),
            pltpu.VMEM((rows_all, LANES), F32),
            dma((3,)),
            dma((BLOCKS,)),
            dma((slots,)),
            dma((slots,)),
            dma((chunks,)),
            dma((chunks,)),
            dma((BLOCKS,)),
            dma((BLOCKS,)),
        ],
        compiler_params=pltpu.CompilerParams(
            collective_id=0, has_side_effects=True, vmem_limit_bytes=60 * 1024 * 1024
        ),
        cost_estimate=pl.CostEstimate(
            flops=2 * rows_all * examples * length, bytes_accessed=2 * examples * length, transcendentals=0
        ),
    )(query_grads, inv_in, inv_out, train_grads[0])


def solution(mesh):
    layers = mesh.shape["layer"]
    return jax.shard_map(
        lambda *args: per_device(layers, *args),
        mesh=mesh,
        in_specs=(
            P(("groups", "layer"), None, None),
            P("layer", None, None),
            P("layer", None, None),
            P("layer", ("groups", "ex"), None),
        ),
        out_specs=P("layer", ("groups", "ex")),
        check_vma=False,
    )
```

```python
import math

import jax
import jax.numpy as jnp
from jax import lax
from jax.experimental import pallas as pl
from jax.experimental.pallas import tpu as pltpu
from jax.sharding import PartitionSpec as P

epsilon = 1e-06
LANES = 128
CHUNK = 16
BLOCKS = 3
MESH = pl.DeviceIdType.MESH
F32 = jnp.float32
BF16 = jnp.bfloat16


def iota(shape, dim):
    return lax.broadcasted_iota(jnp.int32, shape, dim)


def dot(a, b):
    return jnp.dot(a, b, preferred_element_type=F32)


def dot_nt(a, b):
    return lax.dot_general(a, b, (((1,), (1,)), ((), ())), preferred_element_type=F32)


def stack(pieces, axis=0):
    return pieces[0] if len(pieces) == 1 else jnp.concatenate(pieces, axis=axis)


def left_weights(factor):
    size = factor.shape[0]
    half = size // 2
    row, col = iota((size, size), 0), iota((size, size), 1)
    low = row < half
    even_first = jnp.where(low, 2 * row, 2 * (row - half) + 1)
    odd_first = jnp.where(low, 2 * row + 1, 2 * (row - half))
    order = (col == even_first).astype(F32).astype(BF16)
    swapped = (col == odd_first).astype(F32).astype(BF16)
    rows = dot(order, factor).astype(BF16)
    return jnp.where(low, dot_nt(rows, order), dot_nt(rows, swapped)).astype(BF16)


def right_weights(factor):
    size = factor.shape[0]
    row, col = iota((2 * size, size), 0), iota((2 * size, size), 1)
    spread = ((row == col) | (row == col + size)).astype(F32).astype(BF16)
    tiled = dot_nt(dot(spread, factor).astype(BF16), spread)
    row, col = iota((2 * size, 2 * size), 0), iota((2 * size, 2 * size), 1)
    return jnp.where((row < size) == (col < size), tiled, 0.0).astype(BF16)


def kernel(
    layers, own, dims,
    query_hbm, left_hbm, right_hbm, train_hbm,
    out_ref,
    query_v, left_v, right_v, train_v, wide, slabs, arrived, plain, cond, scores, sent, got, norm_high, norm_low,
    local_sem, train_sem, q_send, q_recv, c_send, c_recv, s_send, s_recv,
):
    groups, slots, per_chunk, chunks, rows_all, block, fold, width, slab_rows = dims
    me = lax.axis_index("layer")
    core = lax.axis_index("ex")

    def wrapped(index):
        return jnp.where(index >= layers, index - layers, index)

    ahead = [wrapped(me + k) for k in range(layers)]
    behind = [wrapped(me + layers - k) for k in range(layers)]

    loads = [
        pltpu.make_async_copy(query_hbm, query_v, local_sem.at[0]),
        pltpu.make_async_copy(left_hbm, left_v, local_sem.at[1]),
        pltpu.make_async_copy(right_hbm, right_v, local_sem.at[2]),
    ]
    for load in loads:
        load.start()
    train_loads = [
        pltpu.make_async_copy(train_hbm.at[pl.ds(b * block, block)], train_v.at[b], train_sem.at[b])
        for b in range(BLOCKS)
    ]

    barrier = pltpu.get_barrier_semaphore()
    for k in range(1, layers):
        pl.semaphore_signal(
            barrier, inc=1, device_id={"layer": ahead[k]}, device_id_type=MESH
        )
    pl.semaphore_signal(barrier, inc=1, device_id={"ex": 1 - core}, device_id_type=MESH)

    loads[0].wait()
    for load in train_loads:
        load.start()
    for r in range(own):
        row = query_v[r].astype(F32)
        for t in range(groups):
            wide[r, pl.ds(t, layers, stride=groups), :] = row[:, t * LANES:(t + 1) * LANES]

    def query_copy(i):
        return pltpu.make_async_remote_copy(
            src_ref=slabs.at[i],
            dst_ref=arrived.at[i],
            send_sem=q_send.at[i],
            recv_sem=q_recv.at[i],
            device_id={"layer": wrapped(me + 2 * i + core)},
            device_id_type=MESH,
        )

    def slab_of(i):
        target = wrapped(me + 2 * i + core)
        start = pl.multiple_of(target * groups, groups)
        return stack([wide[r, pl.ds(start, groups), :] for r in range(own)], axis=1).astype(BF16)

    for i in range(slots):
        slabs[i] = slab_of(i)
        if i == 0:
            pl.semaphore_wait(barrier, layers)

            @pl.when(core == 0)
            def _():
                arrived[0] = slabs[0]

            @pl.when(core != 0)
            def _():
                query_copy(0).start()
        else:
            query_copy(i).start()

    loads[1].wait()
    loads[2].wait()
    left = left_weights(left_v[0])
    right = right_weights(right_v[0])
    low = iota((groups, LANES), 1) < LANES // 2

    def cond_copy(j):
        place = core * chunks + j
        return pltpu.make_async_remote_copy(
            src_ref=cond.at[place],
            dst_ref=cond.at[place],
            send_sem=c_send.at[j],
            recv_sem=c_recv.at[j],
            device_id={"ex": 1 - core},
            device_id_type=MESH,
        )

    for j in range(chunks):
        pieces = []
        for i in range(j * per_chunk, (j + 1) * per_chunk):
            if i == 0:
                @pl.when(core != 0)
                def _():
                    query_copy(0).wait_recv()
            else:
                query_copy(i).wait_recv()
            slab = arrived[i].astype(F32)
            for r in range(own):
                piece = slab[:, r * LANES:(r + 1) * LANES]
                pieces.append(stack([piece, pltpu.roll(piece, LANES // 2, 1)], axis=0))
        both = dot(left, stack(pieces, axis=1).astype(BF16))
        mixed = stack(
            [
                jnp.where(low, both[:groups, n * LANES:(n + 1) * LANES], both[groups:, n * LANES:(n + 1) * LANES])
                for n in range(CHUNK)
            ],
            axis=0,
        ).astype(BF16)
        plain[...] = dot(mixed, right)
        place = core * chunks + j
        for t in range(groups):
            cond[place, :, t * LANES:(t + 1) * LANES] = plain[pl.ds(t, CHUNK, stride=groups), :].astype(BF16)
        cond_copy(j).start()

    for j in range(chunks):
        pltpu.make_async_remote_copy(
            src_ref=cond.at[(1 - core) * chunks + j],
            dst_ref=cond.at[(1 - core) * chunks + j],
            send_sem=c_send.at[j],
            recv_sem=c_recv.at[j],
            device_id={"ex": 1 - core},
            device_id_type=MESH,
        ).wait_recv()

    def rows_of(k):
        return (k % 2) * (rows_all // 2) + (k // 2) * own

    def score_copy(b, k):
        return pltpu.make_async_remote_copy(
            src_ref=sent.at[b, k, :, pl.ds(0, width + LANES if b == 0 else width)],
            dst_ref=got.at[b, k, :, pl.ds(0, width + LANES if b == 0 else width)],
            send_sem=s_send.at[b],
            recv_sem=s_recv.at[b],
            device_id={"layer": behind[k]},
            device_id_type=MESH,
        )

    def wait_all(buffer, b, sem):
        others = buffer.at[b, pl.ds(1, layers - 1), :, pl.ds(0, width + LANES if b == 0 else width)]
        pltpu.make_async_copy(others, others, sem.at[b]).wait()

    for i in range(slots):
        if i == 0:
            @pl.when(core != 0)
            def _():
                query_copy(0).wait_send()
        else:
            query_copy(i).wait_send()

    for b in range(BLOCKS):
        train_loads[b].wait()
        queries = cond[...].reshape(rows_all, groups * LANES)
        scores[b] = dot_nt(queries, train_v[b])
        if b == 0:
            total = jnp.zeros((rows_all, LANES), F32)
            for t in range(groups):
                piece = queries[:, t * LANES:(t + 1) * LANES].astype(F32)
                total = total + piece * piece
            norms = jnp.broadcast_to(jnp.sum(total, axis=1, keepdims=True), (rows_all, LANES))
            high = norms.astype(BF16).astype(F32)
            norm_high[...] = high
            norm_low[...] = norms - high
        for k in range(1, layers):
            rows = pl.ds(rows_of(k), own)
            value = scores[b, rows, :]
            parts = [value[:, f * width:(f + 1) * width] for f in range(fold)]
            if own * fold < slab_rows:
                parts.append(jnp.zeros((slab_rows - own * fold, width), F32))
            sent[b, k, :, :width] = stack(parts, axis=0).astype(BF16)
            if b == 0:
                parts = [norm_high[rows, :], norm_low[rows, :]]
                if own * 2 < slab_rows:
                    parts.append(jnp.zeros((slab_rows - own * 2, LANES), F32))
                sent[b, k, :, width:] = stack(parts, axis=0).astype(BF16)
            score_copy(b, k).start()

    for j in range(chunks):
        cond_copy(j).wait_send()
    for b in range(BLOCKS):
        wait_all(got, b, s_recv)
        if b == 0:
            pair = jnp.zeros((slab_rows, LANES), F32)
            for k in range(1, layers):
                pair = pair + got[0, k, :, width:].astype(F32)
            norm = norm_high[:own] + norm_low[:own] + pair[:own] + pair[own:2 * own]
            scale = jnp.sqrt(norm[:, :1] + epsilon)
        summed = jnp.zeros((slab_rows, width), F32)
        for k in range(1, layers):
            summed = summed + got[b, k, :, :width].astype(F32)
        flat = stack([summed[f * own:(f + 1) * own] for f in range(fold)], axis=1)
        out_ref[:, b * block:(b + 1) * block] = (flat + scores[b, pl.ds(0, own), :]) / scale
        wait_all(sent, b, s_send)


def per_device(layers, query_grads, inv_in, inv_out, train_grads):
    own, _, length = query_grads.shape
    examples = train_grads.shape[1]
    groups = length // LANES
    slots = layers // 2
    per_chunk = CHUNK // own
    rows_all = own * layers
    chunks = rows_all // 2 // CHUNK
    block = examples // BLOCKS
    fold = math.gcd(max(1, CHUNK // own), block // LANES)
    width = block // fold
    slab_rows = max(CHUNK, own * fold, own * 2)
    dims = (groups, slots, per_chunk, chunks, rows_all, block, fold, width, slab_rows)
    any_space = pl.BlockSpec(memory_space=pltpu.HBM)
    in_vmem = pl.BlockSpec(memory_space=pltpu.VMEM)
    dma = pltpu.SemaphoreType.DMA
    return pl.pallas_call(
        lambda *refs: kernel(layers, own, dims, *refs),
        out_shape=jax.ShapeDtypeStruct((own, examples), F32),
        in_specs=[any_space] * 4,
        out_specs=in_vmem,
        scratch_shapes=[
            pltpu.VMEM(query_grads.shape, BF16),
            pltpu.VMEM(inv_in.shape, BF16),
            pltpu.VMEM(inv_out.shape, BF16),
            pltpu.VMEM((BLOCKS, block, length), BF16),
            pltpu.VMEM((own, layers * groups, LANES), F32),
            pltpu.VMEM((slots, groups, own * LANES), BF16),
            pltpu.VMEM((slots, groups, own * LANES), BF16),
            pltpu.VMEM((CHUNK * groups, LANES), F32),
            pltpu.VMEM((2 * chunks, CHUNK, length), BF16),
            pltpu.VMEM((BLOCKS, rows_all, block), F32),
            pltpu.VMEM((BLOCKS, layers, slab_rows, width + LANES), BF16),
            pltpu.VMEM((BLOCKS, layers, slab_rows, width + LANES), BF16),
            pltpu.VMEM((rows_all, LANES), F32),
            pltpu.VMEM((rows_all, LANES), F32),
            dma((3,)),
            dma((BLOCKS,)),
            dma((slots,)),
            dma((slots,)),
            dma((chunks,)),
            dma((chunks,)),
            dma((BLOCKS,)),
            dma((BLOCKS,)),
        ],
        compiler_params=pltpu.CompilerParams(
            collective_id=0, has_side_effects=True, vmem_limit_bytes=56 * 1024 * 1024
        ),
        cost_estimate=pl.CostEstimate(
            flops=2 * rows_all * examples * length, bytes_accessed=2 * examples * length, transcendentals=0
        ),
    )(query_grads, inv_in, inv_out, train_grads[0])


def solution(mesh):
    layers = mesh.shape["layer"]
    return jax.shard_map(
        lambda *args: per_device(layers, *args),
        mesh=mesh,
        in_specs=(
            P(("groups", "layer"), None, None),
            P("layer", None, None),
            P("layer", None, None),
            P("layer", ("groups", "ex"), None),
        ),
        out_specs=P("layer", ("groups", "ex")),
        check_vma=False,
    )
```
